32 devices in a mesh: row: 4 (over y, x), col: 8 (over z, core).
Axes of the slice: x: 2, y: 2, z: 4, core: 2. Of those that a mesh axis runs over, the one named last changes fastest.
Arguments:
- matrix: float32 [16384, 16384], P('row', 'col'), may hold values from -85 to 723.7488, as said below
Outputs:
- reduced: float32 [16384, 16384], P('row', 'col')
The draws below stay inside these ranges and needn't reach their ends.
Inputs may be any that keep to these rules, and one draw needn't show every extreme that they name: matrix is symmetric; entry (64 + j, j) and its mirror exceed the other entries of their columns many times over, so that the leading entry of every panel column stays positive through the reflections.
All inputs are finite; a program needn't handle non-finite values.
Results may differ from the reference program's by a relative error of at most 0.00011.
Values sent between devices are 32-bit elements; how exact they have to be, the bound alone decides.
A program may use at most 192 MiB of HBM per device.

```python
import jax
import jax.numpy as jnp
from jax import lax

N = 16384
B = 64


def draw_matrix(key, part):
    key = jax.random.fold_in(key, 11)
    base_key, scale_key = jax.random.split(key)
    base = jnp.clip(jax.random.normal(base_key, (N, N), jnp.float32), -6.0, 6.0)
    scales = jnp.exp(jax.random.uniform(scale_key, (N,), jnp.float32, 0.0, 1.1512925))
    mirrored = (base + base.T) * 0.70710678
    row_ids = jnp.arange(N, dtype=jnp.int32)[:, None]
    col_ids = jnp.arange(N, dtype=jnp.int32)[None, :]
    band = (row_ids == col_ids + B) & (col_ids < B) | (col_ids == row_ids + B) & (row_ids < B)
    leading = 5.0 * jnp.sqrt(jnp.float32(N - B))
    values = scales[:, None] * scales[None, :] * mirrored + jnp.where(band, leading, 0.0)
    return values.astype(jnp.float32)


def setup_inputs(seed: int = 0) -> dict:
    arg_keys = jax.random.split(jax.random.key(seed), 2)
    return {
        "matrix": draw_matrix(jax.random.fold_in(arg_keys[1], 71), 0),
    }


highest = lax.Precision.HIGHEST

def apply_reflector(working, vectors, masked, chosen, totals, pivot_row, index):
    square_sum = totals[index]
    leading = pivot_row[index]
    norm_value = jnp.sqrt(square_sum)
    vector = masked + norm_value * chosen
    tau_value = 2.0 / (2.0 * square_sum + 2.0 * leading * norm_value)
    working = working - tau_value * jnp.outer(vector, totals + norm_value * pivot_row)
    column_mark = (jnp.arange(B, dtype=jnp.int32) == index).astype(working.dtype)
    vectors = vectors + jnp.outer(vector, column_mark)
    return (working, vectors)

def reflectors(panel_cols):
    rows_all = jnp.arange(panel_cols.shape[0], dtype=jnp.int32)

    def reflect_step(index, state):
        working, vectors = state
        column = lax.dynamic_slice_in_dim(working, index, 1, 1)[:, 0]
        masked = jnp.where(rows_all >= index, column, jnp.zeros_like(column))
        chosen = (rows_all == index).astype(working.dtype)
        totals = jnp.dot(masked, working, precision=highest)
        pivot_row = jnp.dot(chosen, working, precision=highest)
        return apply_reflector(working, vectors, masked, chosen, totals, pivot_row, index)
    start = (panel_cols, jnp.zeros_like(panel_cols))
    return lax.fori_loop(0, B, reflect_step, start)[1]

def compact_factor(gram_matrix):
    width = gram_matrix.shape[0]
    upper_part = jnp.triu(gram_matrix, 1) + 0.5 * jnp.diag(jnp.diag(gram_matrix))
    return jax.scipy.linalg.solve_triangular(upper_part, jnp.eye(width, dtype=gram_matrix.dtype), lower=False)

def reference(matrix):
    vectors = reflectors(matrix[B:, :B])
    full = jnp.concatenate([jnp.zeros((B, B), matrix.dtype), vectors], axis=0)
    gram_matrix = jnp.dot(full.T, full, precision=highest)
    compact = compact_factor(gram_matrix)
    image = jnp.dot(matrix, full, precision=highest)
    core = jnp.dot(full.T, image, precision=highest)
    scaled = jnp.dot(image, compact, precision=highest)
    middle = jnp.dot(jnp.dot(compact.T, core, precision=highest), compact, precision=highest)
    updates = scaled - 0.5 * jnp.dot(full, middle, precision=highest)
    return matrix - jnp.dot(full, updates.T, precision=highest) - jnp.dot(updates, full.T, precision=highest)
```

```python
import jax
import jax.numpy as jnp
from jax import lax
from jax.experimental import pallas as pl
from jax.experimental.pallas import tpu as pltpu
from jax.sharding import PartitionSpec as P

B = 64

highest = lax.Precision.HIGHEST
high = lax.Precision.HIGH


def dot(left, right, dims, precision=high):
    return lax.dot_general(
        left, right, (dims, ((), ())), precision=precision, preferred_element_type=jnp.float32
    )


def factor_kernel(small_ref, upper_ref, inner_ref):
    lane = lax.broadcasted_iota(jnp.int32, (B, 2 * B), 1)
    sub = lax.broadcasted_iota(jnp.int32, (B, 2 * B), 0)
    left = lane < B
    shifted_eye = (lane == sub + B).astype(jnp.float32)
    both = small_ref[...]
    swapped = jnp.concatenate([both[:, B:], both[:, :B]], axis=1)
    grams = jnp.where(left, both, shifted_eye)
    pivots = jnp.where(left, swapped, shifted_eye)
    left_row = left[:1]
    factors = jnp.zeros((B, 2 * B), jnp.float32)
    for j in range(B):
        here = sub == j
        row = grams[j : j + 1, :]
        scale = lax.rsqrt(row[:, j : j + 1])
        scaled = row * scale
        grams = grams - (grams[:, j : j + 1] * scale) * scaled
        factors = jnp.where(here, scaled, factors)
        line = pivots[j : j + 1, :] + jnp.where(left_row, scaled, 0.0)
        line = line / line[:, j : j + 1]
        pivots = jnp.where(here, line, pivots - pivots[:, j : j + 1] * line)
    upper = (lane >= sub)[:, :B]
    upper_ref[...] = jnp.where(upper, factors[:, :B], 0.0)
    inner_ref[...] = dot(factors[:, B:], pivots[:, B:], ((0,), (1,)), highest)


def factor(small):
    shape = jax.ShapeDtypeStruct((B, B), jnp.float32)
    return pl.pallas_call(
        factor_kernel,
        out_shape=(shape, shape),
        cost_estimate=pl.CostEstimate(flops=30_000_000, bytes_accessed=65536, transcendentals=0),
    )(small)


def on_device(matrix):
    rows_dev, cols_dev = matrix.shape
    row_pos = lax.axis_index("row")
    col_pos = lax.axis_index("col")
    first_row = row_pos == 0
    first_col = col_pos == 0
    strip_rows = lax.psum(jnp.where(first_col, matrix[:, : 2 * B], 0.0), "col")
    strip_cols = lax.psum(jnp.where(first_row, matrix[: 2 * B, :], 0.0), "row")
    row_ids = row_pos * rows_dev + jnp.arange(rows_dev, dtype=jnp.int32)
    col_ids = col_pos * cols_dev + jnp.arange(cols_dev, dtype=jnp.int32)
    panel_rows = jnp.where((row_ids >= B)[:, None], strip_rows[:, :B], 0.0)
    panel_cols = jnp.where((col_ids >= B)[None, :], strip_cols[:B, :], 0.0)
    top = jnp.where(first_row, strip_rows[B : 2 * B, :], 0.0)
    gram = dot(panel_rows, panel_rows, ((0,), (0,)), highest)
    small = lax.psum(jnp.concatenate([gram, top], axis=1), "row")
    part_rows = dot(matrix, panel_cols, ((1,), (1,)))
    part_cols = dot(panel_rows, matrix, ((0,), (0,)))
    image_rows = lax.psum(part_rows, "col")
    image_cols = lax.psum(part_cols, "row")
    core_part = dot(panel_rows, part_rows, ((0,), (0,)))
    edge_part = jnp.where(first_row, part_rows[B : 2 * B, :], 0.0)
    cores = lax.psum(jnp.concatenate([core_part, edge_part], axis=1), ("row", "col"))
    upper, inner = factor(small[:, : 2 * B])
    corner = small[:, 2 * B :]
    edge = dot(upper, cores[:, B:], ((0,), (0,)), highest)
    core = cores[:, :B] + edge + edge.T + dot(
        upper, dot(corner, upper, ((1,), (0,)), highest), ((0,), (0,)), highest
    )
    middle = 0.5 * dot(inner, dot(core, inner, ((1,), (0,)), highest), ((0,), (0,)), highest)
    pad_rows = jnp.where(first_row, upper, 0.0)
    pad_cols = jnp.where(first_col, upper.T, 0.0)
    basis_rows = panel_rows.at[B : 2 * B, :].add(pad_rows)
    basis_cols = panel_cols.at[:, B : 2 * B].add(pad_cols)
    image_rows = image_rows + dot(strip_rows[:, B:], upper, ((1,), (0,)))
    image_cols = image_cols + dot(upper, strip_cols[B:, :], ((0,), (0,)))
    update_rows = dot(image_rows, inner, ((1,), (0,))) - dot(basis_rows, middle, ((1,), (0,)))
    update_cols = dot(inner, image_cols, ((0,), (0,))) - dot(middle, basis_cols, ((0,), (0,)))
    lefts = jnp.concatenate([basis_rows, update_rows], axis=1)
    rights = jnp.concatenate([update_cols, basis_cols], axis=0)
    return matrix - dot(lefts, rights, ((1,), (0,)))


def solution(mesh):
    placed = (P("row", "col"),)
    return jax.shard_map(
        on_device, mesh=mesh, in_specs=placed, out_specs=P("row", "col"), check_vma=False
    )
```

```python
import functools
import math

import jax
import jax.numpy as jnp
from jax import lax
from jax.experimental import pallas as pl
from jax.experimental.pallas import tpu as pltpu
from jax.sharding import PartitionSpec as P

B = 64

highest = lax.Precision.HIGHEST
high = lax.Precision.HIGH


def dot(left, right, dims, precision=high):
    return lax.dot_general(
        left, right, (dims, ((), ())), precision=precision, preferred_element_type=jnp.float32
    )


def factor_kernel(small_ref, upper_ref, inner_ref):
    lane = lax.broadcasted_iota(jnp.int32, (B, 2 * B), 1)
    sub = lax.broadcasted_iota(jnp.int32, (B, 2 * B), 0)
    left = lane < B
    shifted_eye = (lane == sub + B).astype(jnp.float32)
    both = small_ref[...]
    swapped = jnp.concatenate([both[:, B:], both[:, :B]], axis=1)
    grams = jnp.where(left, both, shifted_eye)
    pivots = jnp.where(left, swapped, shifted_eye)
    left_row = left[:1]
    factors = jnp.zeros((B, 2 * B), jnp.float32)
    for j in range(B):
        here = sub == j
        row = grams[j : j + 1, :]
        scale = lax.rsqrt(row[:, j : j + 1])
        scaled = row * scale
        grams = grams - (grams[:, j : j + 1] * scale) * scaled
        factors = jnp.where(here, scaled, factors)
        line = pivots[j : j + 1, :] + jnp.where(left_row, scaled, 0.0)
        line = line / line[:, j : j + 1]
        pivots = jnp.where(here, line, pivots - pivots[:, j : j + 1] * line)
    upper = (lane >= sub)[:, :B]
    upper_ref[...] = jnp.where(upper, factors[:, :B], 0.0)
    inner_ref[...] = dot(factors[:, B:], pivots[:, B:], ((0,), (1,)), highest)


def factor(small):
    shape = jax.ShapeDtypeStruct((B, B), jnp.float32)
    return pl.pallas_call(
        factor_kernel,
        out_shape=(shape, shape),
        cost_estimate=pl.CostEstimate(flops=30_000_000, bytes_accessed=65536, transcendentals=0),
    )(small)


MESH = pl.DeviceIdType.MESH


def exchange_kernel(n_row, n_col, blocks, pieces, own, *refs):
    if own:
        part_ref, total_ref, wide_ref, small_ref, *refs = refs
        other_ref = None
    else:
        part_ref, other_ref, total_ref, wide_ref, small_ref, *refs = refs
    slots, smalls, rs_send, rs_recv, ag_send, ag_recv, sm_send, sm_recv, ch_send, ch_recv = refs
    row = lax.axis_index("row")
    col = lax.axis_index("col")
    width = part_ref.shape[1]
    lane_parts = math.gcd(n_row, width // 128)
    sub_size = B * lane_parts // n_row
    lane_size = width // lane_parts

    barrier = pltpu.get_barrier_semaphore()
    for k in range(1, n_row):
        pl.semaphore_signal(
            barrier, inc=1, device_id={"row": lax.rem(row + k, n_row)}, device_id_type=MESH
        )
    for k in range(1, n_col):
        pl.semaphore_signal(
            barrier, inc=1, device_id={"col": lax.rem(col + k, n_col)}, device_id_type=MESH
        )
    pl.semaphore_wait(barrier, n_row + n_col - 2)

    def chunk(ref, j):
        sub = pl.multiple_of((j // lane_parts) * sub_size, sub_size)
        lanes = pl.multiple_of(lax.rem(j, lane_parts) * lane_size, lane_size)
        return ref.at[pl.ds(sub, sub_size), pl.ds(lanes, lane_size)]

    scatters = []
    for k in range(1, n_row):
        peer = lax.rem(row + k, n_row)
        copy = pltpu.make_async_remote_copy(
            src_ref=chunk(part_ref, peer),
            dst_ref=slots.at[k - 1],
            send_sem=rs_send.at[k - 1],
            recv_sem=rs_recv.at[k - 1],
            device_id={"row": peer},
            device_id_type=MESH,
        )
        copy.start()
        scatters.append(copy)
    added = chunk(part_ref, row)[...]
    for k in range(1, n_row):
        scatters[k - 1].wait_recv()
        added = added + slots[k - 1]
    mine = chunk(total_ref, row)
    mine[...] = added
    gathers = []
    for k in range(1, n_row):
        copy = pltpu.make_async_remote_copy(
            src_ref=mine,
            dst_ref=mine,
            send_sem=ag_send.at[k - 1],
            recv_sem=ag_recv.at[k - 1],
            device_id={"row": lax.rem(row + k, n_row)},
            device_id_type=MESH,
        )
        copy.start()
        gathers.append(copy)
    for k in range(1, n_row):
        source = lax.rem(row + n_row - k, n_row)
        pltpu.make_async_remote_copy(
            src_ref=mine,
            dst_ref=chunk(total_ref, source),
            send_sem=ag_send.at[k - 1],
            recv_sem=ag_recv.at[k - 1],
            device_id={"row": source},
            device_id_type=MESH,
        ).wait_recv()

    chip, core = col // 2, lax.rem(col, 2)
    partner = col + 1 - 2 * core
    last = n_col // 2 - 1
    piece = width // pieces

    def hand(i, m, way, target):
        view = wide_ref.at[:, pl.ds(i * width + m * piece, piece)]
        return pltpu.make_async_remote_copy(
            src_ref=view,
            dst_ref=view,
            send_sem=ch_send.at[way, i, m],
            recv_sem=ch_recv.at[i, m],
            device_id={"col": target},
            device_id_type=MESH,
        )

    places = []
    for i in range(blocks):
        source = blocks * row + i
        carries = core == lax.rem(source, 2)
        start = source // 2
        up = carries & (chip >= start) & (chip < last)
        down = carries & (chip <= start) & (chip > 0)
        places.append((source, carries, start, up, down))

    def pass_on(i, m):
        _, _, _, up, down = places[i]

        @pl.when(up)
        def _():
            hand(i, m, 0, jnp.minimum(col + 2, n_col - 1)).start()

        @pl.when(down)
        def _():
            hand(i, m, 1, jnp.maximum(col - 2, 0)).start()

        hand(i, m, 2, partner).start()

    for i in range(blocks):

        @pl.when(col == places[i][0])
        def _(i=i):
            wide_ref[:, i * width : (i + 1) * width] = total_ref[...]
            for m in range(pieces):
                pass_on(i, m)

    total = total_ref[...]
    gram = dot(total, total if own else other_ref[...], ((1,), (1,)), highest)
    top = jnp.where(col == 0, total[:, B : 2 * B], 0.0)
    smalls[0] = jnp.concatenate([gram, top], axis=1)
    sends = []
    for k in range(1, n_col):
        copy = pltpu.make_async_remote_copy(
            src_ref=smalls.at[0],
            dst_ref=smalls.at[k],
            send_sem=sm_send.at[k - 1],
            recv_sem=sm_recv.at[k - 1],
            device_id={"col": lax.rem(col + k, n_col)},
            device_id_type=MESH,
        )
        copy.start()
        sends.append(copy)

    for m in range(pieces):
        for i in range(blocks):

            @pl.when(places[i][1] & (col != places[i][0]))
            def _(i=i, m=m):
                hand(i, m, 2, partner).wait_recv()
                pass_on(i, m)

    for copy in sends:
        copy.wait_recv()
    small_ref[...] = jnp.zeros_like(small_ref)

    def add_small(j, carry):
        slot = lax.rem(col + n_col - j, n_col)
        small_ref[...] += smalls[slot]
        return carry

    lax.fori_loop(0, n_col, add_small, 0)
    for i in range(blocks):
        _, carries, _, up, down = places[i]
        for m in range(pieces):

            @pl.when(jnp.logical_not(carries))
            def _(i=i, m=m):
                hand(i, m, 2, partner).wait_recv()

            @pl.when(up)
            def _(i=i, m=m):
                hand(i, m, 0, partner).wait_send()

            @pl.when(down)
            def _(i=i, m=m):
                hand(i, m, 1, partner).wait_send()

            @pl.when(carries)
            def _(i=i, m=m):
                hand(i, m, 2, partner).wait_send()

    for copy in scatters + gathers + sends:
        copy.wait_send()


def exchange(n_row, n_col, identifier, part, other=None):
    width = part.shape[1]
    blocks = n_col // n_row
    pieces = max(1, min(4, width // 256))
    lane_parts = math.gcd(n_row, width // 128)
    chunk = (B * lane_parts // n_row, width // lane_parts)
    dma = pltpu.SemaphoreType.DMA
    args = (part,) if other is None else (part, other)
    whole = pl.BlockSpec(memory_space=pltpu.VMEM)
    return pl.pallas_call(
        functools.partial(exchange_kernel, n_row, n_col, blocks, pieces, other is None),
        out_shape=(
            jax.ShapeDtypeStruct((B, width), jnp.float32),
            jax.ShapeDtypeStruct((B, blocks * width), jnp.float32),
            jax.ShapeDtypeStruct((B, 2 * B), jnp.float32),
        ),
        in_specs=[whole] * len(args),
        out_specs=(whole,) * 3,
        scratch_shapes=[
            pltpu.VMEM((n_row - 1,) + chunk, jnp.float32),
            pltpu.VMEM((n_col, B, 2 * B), jnp.float32),
            dma((n_row - 1,)),
            dma((n_row - 1,)),
            dma((n_row - 1,)),
            dma((n_row - 1,)),
            dma((n_col - 1,)),
            dma((n_col - 1,)),
            dma((3, blocks, pieces)),
            dma((blocks, pieces)),
        ],
        compiler_params=pltpu.CompilerParams(
            collective_id=identifier, has_side_effects=True, vmem_limit_bytes=24 << 20
        ),
    )(*args)


def on_device(n_row, n_col, matrix):
    rows_dev, cols_dev = matrix.shape
    first_row = lax.axis_index("row") == 0
    first_col = lax.axis_index("col") == 0
    after = first_row & (
        lax.axis_index("col") * cols_dev + jnp.arange(cols_dev, dtype=jnp.int32) >= B
    )
    share = functools.partial(exchange, n_row, n_col)
    panel_cols, panel_rows, small = share(0, jnp.where(after[None, :], matrix[:B, :], 0.0))
    small = jnp.concatenate([small[:, :B], small[:, B:].T], axis=1)
    upper, inner = factor(small)
    lower = upper.T
    basis_rows = panel_rows.at[:, B : 2 * B].add(jnp.where(first_row, lower, 0.0))
    basis_cols = panel_cols.at[:, B : 2 * B].add(jnp.where(first_col, lower, 0.0))
    image_part = dot(basis_rows, matrix, ((1,), (0,)))
    image_cols, image_rows, small = share(1, image_part, basis_cols)
    core = small[:, :B]
    middle = 0.5 * dot(inner, dot(core, inner, ((1,), (0,)), highest), ((0,), (0,)), highest)

    def updates(image, basis):
        return dot(inner, image, ((0,), (0,))) - dot(middle, basis, ((0,), (0,)))

    lefts = jnp.concatenate([basis_rows, updates(image_rows, basis_rows)], axis=0)
    rights = jnp.concatenate([updates(image_cols, basis_cols), basis_cols], axis=0)
    return matrix - dot(lefts, rights, ((0,), (0,)))


def solution(mesh):
    placed = (P("row", "col"),)
    return jax.shard_map(
        functools.partial(on_device, mesh.shape["row"], mesh.shape["col"]),
        mesh=mesh,
        in_specs=placed,
        out_specs=P("row", "col"),
        check_vma=False,
    )
```

```python
import functools
import math

import jax
import jax.numpy as jnp
from jax import lax
from jax.experimental import pallas as pl
from jax.experimental.pallas import tpu as pltpu
from jax.sharding import PartitionSpec as P

B = 64

highest = lax.Precision.HIGHEST
high = lax.Precision.HIGH


def dot(left, right, dims, precision=high):
    return lax.dot_general(
        left, right, (dims, ((), ())), precision=precision, preferred_element_type=jnp.float32
    )


def factor_kernel(small_ref, upper_ref, inner_ref):
    lane = lax.broadcasted_iota(jnp.int32, (B, 2 * B), 1)
    sub = lax.broadcasted_iota(jnp.int32, (B, 2 * B), 0)
    left = lane < B
    shifted_eye = (lane == sub + B).astype(jnp.float32)
    both = small_ref[...]
    swapped = jnp.concatenate([both[:, B:], both[:, :B]], axis=1)
    grams = jnp.where(left, both, shifted_eye)
    pivots = jnp.where(left, swapped, shifted_eye)
    left_row = left[:1]
    factors = jnp.zeros((B, 2 * B), jnp.float32)
    for j in range(B):
        here = sub == j
        row = grams[j : j + 1, :]
        scale = lax.rsqrt(row[:, j : j + 1])
        scaled = row * scale
        grams = grams - (grams[:, j : j + 1] * scale) * scaled
        factors = jnp.where(here, scaled, factors)
        line = pivots[j : j + 1, :] + jnp.where(left_row, scaled, 0.0)
        line = line / line[:, j : j + 1]
        pivots = jnp.where(here, line, pivots - pivots[:, j : j + 1] * line)
    upper = (lane >= sub)[:, :B]
    upper_ref[...] = jnp.where(upper, factors[:, :B], 0.0)
    inner_ref[...] = dot(factors[:, B:], pivots[:, B:], ((0,), (1,)), highest)


def factor(small):
    shape = jax.ShapeDtypeStruct((B, B), jnp.float32)
    return pl.pallas_call(
        factor_kernel,
        out_shape=(shape, shape),
        cost_estimate=pl.CostEstimate(flops=30_000_000, bytes_accessed=65536, transcendentals=0),
    )(small)


MESH = pl.DeviceIdType.MESH


def exchange_kernel(n_row, n_col, blocks, pieces, own, *refs):
    if own:
        part_ref, total_ref, wide_ref, small_ref, *refs = refs
        other_ref = None
    else:
        part_ref, other_ref, total_ref, wide_ref, small_ref, *refs = refs
    slots, smalls, rs_send, rs_recv, ag_send, ag_recv, sm_send, sm_recv, ch_send, ch_recv = refs
    row = lax.axis_index("row")
    col = lax.axis_index("col")
    width = part_ref.shape[1]
    lane_parts = math.gcd(n_row, width // 128)
    sub_size = B * lane_parts // n_row
    lane_size = width // lane_parts

    barrier = pltpu.get_barrier_semaphore()
    for k in range(1, n_row):
        pl.semaphore_signal(
            barrier, inc=1, device_id={"row": lax.rem(row + k, n_row)}, device_id_type=MESH
        )
    for k in range(1, n_col):
        pl.semaphore_signal(
            barrier, inc=1, device_id={"col": lax.rem(col + k, n_col)}, device_id_type=MESH
        )
    pl.semaphore_wait(barrier, n_row + n_col - 2)

    def chunk(ref, j):
        sub = pl.multiple_of((j // lane_parts) * sub_size, sub_size)
        lanes = pl.multiple_of(lax.rem(j, lane_parts) * lane_size, lane_size)
        return ref.at[pl.ds(sub, sub_size), pl.ds(lanes, lane_size)]

    scatters = []
    for k in range(1, n_row):
        peer = lax.rem(row + k, n_row)
        copy = pltpu.make_async_remote_copy(
            src_ref=chunk(part_ref, peer),
            dst_ref=slots.at[k - 1],
            send_sem=rs_send.at[k - 1],
            recv_sem=rs_recv.at[k - 1],
            device_id={"row": peer},
            device_id_type=MESH,
        )
        copy.start()
        scatters.append(copy)
    added = chunk(part_ref, row)[...]
    for k in range(1, n_row):
        scatters[k - 1].wait_recv()
        added = added + slots[k - 1]
    mine = chunk(total_ref, row)
    mine[...] = added
    gathers = []
    for k in range(1, n_row):
        copy = pltpu.make_async_remote_copy(
            src_ref=mine,
            dst_ref=mine,
            send_sem=ag_send.at[k - 1],
            recv_sem=ag_recv.at[k - 1],
            device_id={"row": lax.rem(row + k, n_row)},
            device_id_type=MESH,
        )
        copy.start()
        gathers.append(copy)
    for k in range(1, n_row):
        source = lax.rem(row + n_row - k, n_row)
        pltpu.make_async_remote_copy(
            src_ref=mine,
            dst_ref=chunk(total_ref, source),
            send_sem=ag_send.at[k - 1],
            recv_sem=ag_recv.at[k - 1],
            device_id={"row": source},
            device_id_type=MESH,
        ).wait_recv()

    chip, core = col // 2, lax.rem(col, 2)
    partner = col + 1 - 2 * core
    last = n_col // 2 - 1
    piece = width // pieces

    def hand(i, m, way, target):
        view = wide_ref.at[:, pl.ds(i * width + m * piece, piece)]
        return pltpu.make_async_remote_copy(
            src_ref=view,
            dst_ref=view,
            send_sem=ch_send.at[way, i, m],
            recv_sem=ch_recv.at[i, m],
            device_id={"col": target},
            device_id_type=MESH,
        )

    places = []
    for i in range(blocks):
        source = blocks * row + i
        carries = core == lax.rem(source, 2)
        start = source // 2
        up = carries & (chip >= start) & (chip < last)
        down = carries & (chip <= start) & (chip > 0)
        places.append((source, carries, start, up, down))

    def pass_on(i, m):
        _, _, _, up, down = places[i]

        @pl.when(up)
        def _():
            hand(i, m, 0, jnp.minimum(col + 2, n_col - 1)).start()

        @pl.when(down)
        def _():
            hand(i, m, 1, jnp.maximum(col - 2, 0)).start()

        hand(i, m, 2, partner).start()

    for i in range(blocks):

        @pl.when(col == places[i][0])
        def _(i=i):
            wide_ref[:, i * width : (i + 1) * width] = total_ref[...]
            for m in range(pieces):
                pass_on(i, m)

    total = total_ref[...]
    gram = dot(total, total if own else other_ref[...], ((1,), (1,)), highest)
    top = jnp.where(col == 0, total[:, B : 2 * B], 0.0)
    smalls[0] = jnp.concatenate([gram, top], axis=1)
    sends = []
    for k in range(1, n_col):
        copy = pltpu.make_async_remote_copy(
            src_ref=smalls.at[0],
            dst_ref=smalls.at[k],
            send_sem=sm_send.at[k - 1],
            recv_sem=sm_recv.at[k - 1],
            device_id={"col": lax.rem(col + k, n_col)},
            device_id_type=MESH,
        )
        copy.start()
        sends.append(copy)

    for m in range(pieces):
        for i in range(blocks):

            @pl.when(places[i][1] & (col != places[i][0]))
            def _(i=i, m=m):
                hand(i, m, 2, partner).wait_recv()
                pass_on(i, m)

    for copy in sends:
        copy.wait_recv()
    small_ref[...] = jnp.zeros_like(small_ref)

    def add_small(j, carry):
        slot = lax.rem(col + n_col - j, n_col)
        small_ref[...] += smalls[slot]
        return carry

    lax.fori_loop(0, n_col, add_small, 0)
    for i in range(blocks):
        _, carries, _, up, down = places[i]
        for m in range(pieces):

            @pl.when(jnp.logical_not(carries))
            def _(i=i, m=m):
                hand(i, m, 2, partner).wait_recv()

            @pl.when(up)
            def _(i=i, m=m):
                hand(i, m, 0, partner).wait_send()

            @pl.when(down)
            def _(i=i, m=m):
                hand(i, m, 1, partner).wait_send()

            @pl.when(carries)
            def _(i=i, m=m):
                hand(i, m, 2, partner).wait_send()

    for copy in scatters + gathers + sends:
        copy.wait_send()


def exchange(n_row, n_col, identifier, part, other=None):
    width = part.shape[1]
    blocks = n_col // n_row
    pieces = min(8, width // 128)
    lane_parts = math.gcd(n_row, width // 128)
    chunk = (B * lane_parts // n_row, width // lane_parts)
    dma = pltpu.SemaphoreType.DMA
    args = (part,) if other is None else (part, other)
    whole = pl.BlockSpec(memory_space=pltpu.VMEM)
    return pl.pallas_call(
        functools.partial(exchange_kernel, n_row, n_col, blocks, pieces, other is None),
        out_shape=(
            jax.ShapeDtypeStruct((B, width), jnp.float32),
            jax.ShapeDtypeStruct((B, blocks * width), jnp.float32),
            jax.ShapeDtypeStruct((B, 2 * B), jnp.float32),
        ),
        in_specs=[whole] * len(args),
        out_specs=(whole,) * 3,
        scratch_shapes=[
            pltpu.VMEM((n_row - 1,) + chunk, jnp.float32),
            pltpu.VMEM((n_col, B, 2 * B), jnp.float32),
            dma((n_row - 1,)),
            dma((n_row - 1,)),
            dma((n_row - 1,)),
            dma((n_row - 1,)),
            dma((n_col - 1,)),
            dma((n_col - 1,)),
            dma((3, blocks, pieces)),
            dma((blocks, pieces)),
        ],
        compiler_params=pltpu.CompilerParams(
            collective_id=identifier, has_side_effects=True, vmem_limit_bytes=24 << 20
        ),
    )(*args)


def halves(values):
    top = values.astype(jnp.bfloat16)
    return top, (values - top.astype(jnp.float32)).astype(jnp.bfloat16)


def image_kernel(basis_ref, matrix_ref, out_ref):
    @pl.when(pl.program_id(0) == 0)
    def _():
        out_ref[...] = jnp.zeros_like(out_ref)

    basis_top, basis_rest = halves(basis_ref[...])
    top, rest = halves(matrix_ref[...])
    both = dot(jnp.concatenate([basis_top, basis_rest], axis=0), top, ((1,), (0,)), None)
    out_ref[...] += both[:B] + both[B:] + dot(basis_top, rest, ((1,), (0,)), None)


def image(basis, matrix):
    rows, cols = matrix.shape
    tile = math.gcd(rows, 256)
    return pl.pallas_call(
        image_kernel,
        grid=(rows // tile,),
        in_specs=[
            pl.BlockSpec((B, tile), lambda i: (0, i)),
            pl.BlockSpec((tile, cols), lambda i: (i, 0)),
        ],
        out_specs=pl.BlockSpec((B, cols), lambda i: (0, 0)),
        out_shape=jax.ShapeDtypeStruct((B, cols), jnp.float32),
        compiler_params=pltpu.CompilerParams(vmem_limit_bytes=32 << 20),
    )(basis, matrix)


def reduce_kernel(
    matrix_ref, basis_rows_ref, image_rows_ref, basis_ref, image_ref, mix_ref, out_ref, rights_ref
):
    def update(image, basis):
        return dot(mix_ref[...], jnp.concatenate([image, basis], axis=0), ((0,), (0,)), highest)

    @pl.when(pl.program_id(0) == 0)
    def _():
        basis = basis_ref[...]
        top, rest = halves(jnp.concatenate([update(image_ref[...], basis), basis], axis=0))
        rights_ref[...] = jnp.concatenate([top, rest, top], axis=0)

    basis = basis_rows_ref[...]
    lefts = jnp.concatenate([basis, update(image_rows_ref[...], basis)], axis=0)
    top, rest = halves(lefts.T)
    lefts = jnp.concatenate([top, top, rest], axis=1)
    out_ref[...] = matrix_ref[...] - dot(lefts, rights_ref[...], ((1,), (0,)), None)


def reduce(matrix, basis_rows, image_rows, basis_cols, image_cols, mix):
    rows, cols = matrix.shape
    tile = math.gcd(rows, 256)
    strip = pl.BlockSpec((B, tile), lambda i: (0, i))
    whole = pl.BlockSpec((B, cols), lambda i: (0, 0))
    return pl.pallas_call(
        reduce_kernel,
        grid=(rows // tile,),
        in_specs=[
            pl.BlockSpec((tile, cols), lambda i: (i, 0)),
            strip,
            strip,
            whole,
            whole,
            pl.BlockSpec((2 * B, B), lambda i: (0, 0)),
        ],
        out_specs=pl.BlockSpec((tile, cols), lambda i: (i, 0)),
        out_shape=jax.ShapeDtypeStruct(matrix.shape, jnp.float32),
        scratch_shapes=[pltpu.VMEM((6 * B, cols), jnp.bfloat16)],
        compiler_params=pltpu.CompilerParams(vmem_limit_bytes=32 << 20),
    )(matrix, basis_rows, image_rows, basis_cols, image_cols, mix)


def on_device(n_row, n_col, matrix):
    rows_dev, cols_dev = matrix.shape
    first_row = lax.axis_index("row") == 0
    first_col = lax.axis_index("col") == 0
    after = first_row & (
        lax.axis_index("col") * cols_dev + jnp.arange(cols_dev, dtype=jnp.int32) >= B
    )
    share = functools.partial(exchange, n_row, n_col)
    panel_cols, panel_rows, small = share(0, jnp.where(after[None, :], matrix[:B, :], 0.0))
    small = jnp.concatenate([small[:, :B], small[:, B:].T], axis=1)
    upper, inner = factor(small)
    lower = upper.T
    basis_rows = panel_rows.at[:, B : 2 * B].add(jnp.where(first_row, lower, 0.0))
    basis_cols = panel_cols.at[:, B : 2 * B].add(jnp.where(first_col, lower, 0.0))
    image_cols, image_rows, small = share(1, image(basis_rows, matrix), basis_cols)
    core = small[:, :B]
    middle = 0.5 * dot(inner, dot(core, inner, ((1,), (0,)), highest), ((0,), (0,)), highest)
    mix = jnp.concatenate([inner, -middle], axis=0)
    return reduce(matrix, basis_rows, image_rows, basis_cols, image_cols, mix)


def solution(mesh):
    placed = (P("row", "col"),)
    return jax.shard_map(
        functools.partial(on_device, mesh.shape["row"], mesh.shape["col"]),
        mesh=mesh,
        in_specs=placed,
        out_specs=P("row", "col"),
        check_vma=False,
    )
```

```python
import functools
import math

import jax
import jax.numpy as jnp
from jax import lax
from jax.experimental import pallas as pl
from jax.experimental.pallas import tpu as pltpu
from jax.sharding import PartitionSpec as P

B = 64

highest = lax.Precision.HIGHEST
high = lax.Precision.HIGH


def dot(left, right, dims, precision=high):
    return lax.dot_general(
        left, right, (dims, ((), ())), precision=precision, preferred_element_type=jnp.float32
    )


def factor_kernel(small_ref, upper_ref, inner_ref):
    lane = lax.broadcasted_iota(jnp.int32, (B, 2 * B), 1)
    sub = lax.broadcasted_iota(jnp.int32, (B, 2 * B), 0)
    left = lane < B
    shifted_eye = (lane == sub + B).astype(jnp.float32)
    both = small_ref[...]
    swapped = jnp.concatenate([both[:, B:], both[:, :B]], axis=1)
    grams = jnp.where(left, both, shifted_eye)
    pivots = jnp.where(left, swapped, shifted_eye)
    left_row = left[:1]
    factors = jnp.zeros((B, 2 * B), jnp.float32)
    for j in range(B):
        here = sub == j
        row = grams[j : j + 1, :]
        scale = lax.rsqrt(row[:, j : j + 1])
        scaled = row * scale
        grams = grams - (grams[:, j : j + 1] * scale) * scaled
        factors = jnp.where(here, scaled, factors)
        line = pivots[j : j + 1, :] + jnp.where(left_row, scaled, 0.0)
        line = line / line[:, j : j + 1]
        pivots = jnp.where(here, line, pivots - pivots[:, j : j + 1] * line)
    upper = (lane >= sub)[:, :B]
    upper_ref[...] = jnp.where(upper, factors[:, :B], 0.0)
    inner_ref[...] = dot(factors[:, B:], pivots[:, B:], ((0,), (1,)), highest)


def factor(small):
    shape = jax.ShapeDtypeStruct((B, B), jnp.float32)
    return pl.pallas_call(
        factor_kernel,
        out_shape=(shape, shape),
        cost_estimate=pl.CostEstimate(flops=30_000_000, bytes_accessed=65536, transcendentals=0),
    )(small)


MESH = pl.DeviceIdType.MESH


def exchange_kernel(n_row, n_col, blocks, pieces, own, *refs):
    if own:
        part_ref, total_ref, wide_ref, small_ref, *refs = refs
        other_ref = None
    else:
        part_ref, other_ref, total_ref, wide_ref, small_ref, *refs = refs
    slots, smalls, rs_send, rs_recv, ag_send, ag_recv, sm_send, sm_recv, ch_send, ch_recv = refs
    row = lax.axis_index("row")
    col = lax.axis_index("col")
    width = part_ref.shape[1]
    lane_parts = math.gcd(n_row, width // 128)
    sub_size = B * lane_parts // n_row
    lane_size = width // lane_parts

    barrier = pltpu.get_barrier_semaphore()
    for k in range(1, n_row):
        pl.semaphore_signal(
            barrier, inc=1, device_id={"row": lax.rem(row + k, n_row)}, device_id_type=MESH
        )
    for k in range(1, n_col):
        pl.semaphore_signal(
            barrier, inc=1, device_id={"col": lax.rem(col + k, n_col)}, device_id_type=MESH
        )
    pl.semaphore_wait(barrier, n_row + n_col - 2)

    def chunk(ref, j):
        sub = pl.multiple_of((j // lane_parts) * sub_size, sub_size)
        lanes = pl.multiple_of(lax.rem(j, lane_parts) * lane_size, lane_size)
        return ref.at[pl.ds(sub, sub_size), pl.ds(lanes, lane_size)]

    scatters = []
    for k in range(1, n_row):
        peer = lax.rem(row + k, n_row)
        copy = pltpu.make_async_remote_copy(
            src_ref=chunk(part_ref, peer),
            dst_ref=slots.at[k - 1],
            send_sem=rs_send.at[k - 1],
            recv_sem=rs_recv.at[k - 1],
            device_id={"row": peer},
            device_id_type=MESH,
        )
        copy.start()
        scatters.append(copy)
    added = chunk(part_ref, row)[...]
    for k in range(1, n_row):
        scatters[k - 1].wait_recv()
        added = added + slots[k - 1]
    mine = chunk(total_ref, row)
    mine[...] = added
    gathers = []
    for k in range(1, n_row):
        copy = pltpu.make_async_remote_copy(
            src_ref=mine,
            dst_ref=mine,
            send_sem=ag_send.at[k - 1],
            recv_sem=ag_recv.at[k - 1],
            device_id={"row": lax.rem(row + k, n_row)},
            device_id_type=MESH,
        )
        copy.start()
        gathers.append(copy)
    chip, core = col // 2, lax.rem(col, 2)
    partner = col + 1 - 2 * core
    last = n_col // 2 - 1
    piece = width // pieces
    streamed = lane_parts == n_row and pieces == n_row

    def place(m):
        return pl.multiple_of((lax.rem(row + n_row - m, n_row) if streamed else m) * piece, piece)

    def hand(i, m, way, target):
        view = wide_ref.at[:, pl.ds(i * width + place(m), piece)]
        return pltpu.make_async_remote_copy(
            src_ref=view,
            dst_ref=view,
            send_sem=ch_send.at[way, i, m],
            recv_sem=ch_recv.at[i, m],
            device_id={"col": target},
            device_id_type=MESH,
        )

    places = []
    for i in range(blocks):
        source = blocks * row + i
        carries = core == lax.rem(source, 2)
        start = source // 2
        up = carries & (chip >= start) & (chip < last)
        down = carries & (chip <= start) & (chip > 0)
        places.append((source, carries, start, up, down))

    def pass_on(i, m):
        _, _, _, up, down = places[i]

        @pl.when(up)
        def _():
            hand(i, m, 0, jnp.minimum(col + 2, n_col - 1)).start()

        @pl.when(down)
        def _():
            hand(i, m, 1, jnp.maximum(col - 2, 0)).start()

        hand(i, m, 2, partner).start()

    def begin(m):
        for i in range(blocks):

            @pl.when(col == places[i][0])
            def _(i=i):
                wide_ref[:, pl.ds(i * width + place(m), piece)] = total_ref[:, pl.ds(place(m), piece)]
                pass_on(i, m)

    if streamed:
        begin(0)
    for k in range(1, n_row):
        source = lax.rem(row + n_row - k, n_row)
        pltpu.make_async_remote_copy(
            src_ref=mine,
            dst_ref=chunk(total_ref, source),
            send_sem=ag_send.at[k - 1],
            recv_sem=ag_recv.at[k - 1],
            device_id={"row": source},
            device_id_type=MESH,
        ).wait_recv()
        if streamed:
            begin(k)
    if not streamed:
        for m in range(pieces):
            begin(m)

    def follow(i, m, chosen):
        @pl.when(chosen)
        def _():
            hand(i, m, 2, partner).wait_recv()
            pass_on(i, m)

    nearest = []
    for i in range(blocks):
        _, carries, start, _, _ = places[i]
        nearest.append(carries & ((chip == start + 1) | (chip == start - 1)))
        follow(i, 0, nearest[i])

    total = total_ref[...]
    gram = dot(total, total if own else other_ref[...], ((1,), (1,)), highest)
    top = jnp.where(col == 0, total[:, B : 2 * B], 0.0)
    smalls[0] = jnp.concatenate([gram, top], axis=1)
    sends = []
    for k in range(1, n_col):
        copy = pltpu.make_async_remote_copy(
            src_ref=smalls.at[0],
            dst_ref=smalls.at[k],
            send_sem=sm_send.at[k - 1],
            recv_sem=sm_recv.at[k - 1],
            device_id={"col": lax.rem(col + k, n_col)},
            device_id_type=MESH,
        )
        copy.start()
        sends.append(copy)

    for m in range(pieces):
        for i in range(blocks):
            rest = places[i][1] & (col != places[i][0])
            follow(i, m, rest & jnp.logical_not(nearest[i]) if m == 0 else rest)

    for copy in sends:
        copy.wait_recv()
    small_ref[...] = jnp.zeros_like(small_ref)

    def add_small(j, carry):
        slot = lax.rem(col + n_col - j, n_col)
        small_ref[...] += smalls[slot]
        return carry

    lax.fori_loop(0, n_col, add_small, 0)
    for i in range(blocks):
        _, carries, _, up, down = places[i]
        for m in range(pieces):

            @pl.when(jnp.logical_not(carries))
            def _(i=i, m=m):
                hand(i, m, 2, partner).wait_recv()

            @pl.when(up)
            def _(i=i, m=m):
                hand(i, m, 0, partner).wait_send()

            @pl.when(down)
            def _(i=i, m=m):
                hand(i, m, 1, partner).wait_send()

            @pl.when(carries)
            def _(i=i, m=m):
                hand(i, m, 2, partner).wait_send()

    for copy in scatters + gathers + sends:
        copy.wait_send()


def exchange(n_row, n_col, identifier, part, other=None):
    width = part.shape[1]
    blocks = n_col // n_row
    pieces = max(1, min(4, width // 256))
    lane_parts = math.gcd(n_row, width // 128)
    chunk = (B * lane_parts // n_row, width // lane_parts)
    dma = pltpu.SemaphoreType.DMA
    args = (part,) if other is None else (part, other)
    whole = pl.BlockSpec(memory_space=pltpu.VMEM)
    return pl.pallas_call(
        functools.partial(exchange_kernel, n_row, n_col, blocks, pieces, other is None),
        out_shape=(
            jax.ShapeDtypeStruct((B, width), jnp.float32),
            jax.ShapeDtypeStruct((B, blocks * width), jnp.float32),
            jax.ShapeDtypeStruct((B, 2 * B), jnp.float32),
        ),
        in_specs=[whole] * len(args),
        out_specs=(whole,) * 3,
        scratch_shapes=[
            pltpu.VMEM((n_row - 1,) + chunk, jnp.float32),
            pltpu.VMEM((n_col, B, 2 * B), jnp.float32),
            dma((n_row - 1,)),
            dma((n_row - 1,)),
            dma((n_row - 1,)),
            dma((n_row - 1,)),
            dma((n_col - 1,)),
            dma((n_col - 1,)),
            dma((3, blocks, pieces)),
            dma((blocks, pieces)),
        ],
        compiler_params=pltpu.CompilerParams(
            collective_id=identifier, has_side_effects=True, vmem_limit_bytes=24 << 20
        ),
    )(*args)


def on_device(n_row, n_col, matrix):
    rows_dev, cols_dev = matrix.shape
    first_row = lax.axis_index("row") == 0
    first_col = lax.axis_index("col") == 0
    after = first_row & (
        lax.axis_index("col") * cols_dev + jnp.arange(cols_dev, dtype=jnp.int32) >= B
    )
    share = functools.partial(exchange, n_row, n_col)
    panel_cols, panel_rows, small = share(0, jnp.where(after[None, :], matrix[:B, :], 0.0))
    small = jnp.concatenate([small[:, :B], small[:, B:].T], axis=1)
    upper, inner = factor(small)
    lower = upper.T
    basis_rows = panel_rows.at[:, B : 2 * B].add(jnp.where(first_row, lower, 0.0))
    basis_cols = panel_cols.at[:, B : 2 * B].add(jnp.where(first_col, lower, 0.0))
    image_part = dot(basis_rows, matrix, ((1,), (0,)))
    image_cols, image_rows, small = share(1, image_part, basis_cols)
    core = small[:, :B]
    middle = 0.5 * dot(inner, dot(core, inner, ((1,), (0,)), highest), ((0,), (0,)), highest)

    def updates(image, basis):
        return dot(inner, image, ((0,), (0,))) - dot(middle, basis, ((0,), (0,)))

    lefts = jnp.concatenate([basis_rows, updates(image_rows, basis_rows)], axis=0)
    rights = jnp.concatenate([updates(image_cols, basis_cols), basis_cols], axis=0)
    return matrix - dot(lefts, rights, ((0,), (0,)))


def solution(mesh):
    placed = (P("row", "col"),)
    return jax.shard_map(
        functools.partial(on_device, mesh.shape["row"], mesh.shape["col"]),
        mesh=mesh,
        in_specs=placed,
        out_specs=P("row", "col"),
        check_vma=False,
    )
```

```python
import functools
import math

import jax
import jax.numpy as jnp
from jax import lax
from jax.experimental import pallas as pl
from jax.experimental.pallas import tpu as pltpu
from jax.sharding import PartitionSpec as P

B = 64

highest = lax.Precision.HIGHEST
high = lax.Precision.HIGH


def dot(left, right, dims, precision=high):
    return lax.dot_general(
        left, right, (dims, ((), ())), precision=precision, preferred_element_type=jnp.float32
    )


def factor_kernel(small_ref, upper_ref, inner_ref):
    lane = lax.broadcasted_iota(jnp.int32, (B, 2 * B), 1)
    sub = lax.broadcasted_iota(jnp.int32, (B, 2 * B), 0)
    left = lane < B
    shifted_eye = (lane == sub + B).astype(jnp.float32)
    both = small_ref[...]
    swapped = jnp.concatenate([both[:, B:], both[:, :B]], axis=1)
    grams = jnp.where(left, both, shifted_eye)
    pivots = jnp.where(left, swapped, shifted_eye)
    left_row = left[:1]
    factors = jnp.zeros((B, 2 * B), jnp.float32)
    for j in range(B):
        here = sub == j
        row = grams[j : j + 1, :]
        scale = lax.rsqrt(row[:, j : j + 1])
        scaled = row * scale
        grams = grams - (grams[:, j : j + 1] * scale) * scaled
        factors = jnp.where(here, scaled, factors)
        line = pivots[j : j + 1, :] + jnp.where(left_row, scaled, 0.0)
        line = line / line[:, j : j + 1]
        pivots = jnp.where(here, line, pivots - pivots[:, j : j + 1] * line)
    upper = (lane >= sub)[:, :B]
    upper_ref[...] = jnp.where(upper, factors[:, :B], 0.0)
    inner_ref[...] = dot(factors[:, B:], pivots[:, B:], ((0,), (1,)), highest)


def factor(small):
    shape = jax.ShapeDtypeStruct((B, B), jnp.float32)
    return pl.pallas_call(
        factor_kernel,
        out_shape=(shape, shape),
        cost_estimate=pl.CostEstimate(flops=30_000_000, bytes_accessed=65536, transcendentals=0),
    )(small)


MESH = pl.DeviceIdType.MESH


def exchange_kernel(n_row, n_col, blocks, pieces, own, *refs):
    if own:
        part_ref, total_ref, wide_ref, small_ref, *refs = refs
        other_ref = None
    else:
        part_ref, other_ref, total_ref, wide_ref, small_ref, *refs = refs
    slots, smalls, rs_send, rs_recv, ag_send, ag_recv, sm_send, sm_recv, ch_send, ch_recv = refs
    row = lax.axis_index("row")
    col = lax.axis_index("col")
    width = part_ref.shape[1]
    lane_parts = math.gcd(n_row, width // 128)
    sub_size = B * lane_parts // n_row
    lane_size = width // lane_parts

    barrier = pltpu.get_barrier_semaphore()
    for k in range(1, n_row):
        pl.semaphore_signal(
            barrier, inc=1, device_id={"row": lax.rem(row + k, n_row)}, device_id_type=MESH
        )
    for k in range(1, n_col):
        pl.semaphore_signal(
            barrier, inc=1, device_id={"col": lax.rem(col + k, n_col)}, device_id_type=MESH
        )
    pl.semaphore_wait(barrier, n_row + n_col - 2)

    def chunk(ref, j):
        sub = pl.multiple_of((j // lane_parts) * sub_size, sub_size)
        lanes = pl.multiple_of(lax.rem(j, lane_parts) * lane_size, lane_size)
        return ref.at[pl.ds(sub, sub_size), pl.ds(lanes, lane_size)]

    scatters = []
    for k in range(1, n_row):
        peer = lax.rem(row + k, n_row)
        copy = pltpu.make_async_remote_copy(
            src_ref=chunk(part_ref, peer),
            dst_ref=slots.at[k - 1],
            send_sem=rs_send.at[k - 1],
            recv_sem=rs_recv.at[k - 1],
            device_id={"row": peer},
            device_id_type=MESH,
        )
        copy.start()
        scatters.append(copy)
    added = chunk(part_ref, row)[...]
    for k in range(1, n_row):
        scatters[k - 1].wait_recv()
        added = added + slots[k - 1]
    mine = chunk(total_ref, row)
    mine[...] = added
    gathers = []
    for k in range(1, n_row):
        copy = pltpu.make_async_remote_copy(
            src_ref=mine,
            dst_ref=mine,
            send_sem=ag_send.at[k - 1],
            recv_sem=ag_recv.at[k - 1],
            device_id={"row": lax.rem(row + k, n_row)},
            device_id_type=MESH,
        )
        copy.start()
        gathers.append(copy)
    chip, core = col // 2, lax.rem(col, 2)
    partner = col + 1 - 2 * core
    last = n_col // 2 - 1
    piece = width // pieces
    streamed = lane_parts == n_row and pieces == 2 * n_row

    def place(m):
        if streamed:
            m = 2 * lax.rem(row + n_row - m // 2, n_row) + m % 2
        return pl.multiple_of(m * piece, piece)

    def hand(i, m, way, target):
        view = wide_ref.at[:, pl.ds(i * width + place(m), piece)]
        return pltpu.make_async_remote_copy(
            src_ref=view,
            dst_ref=view,
            send_sem=ch_send.at[way, i, m],
            recv_sem=ch_recv.at[i, m],
            device_id={"col": target},
            device_id_type=MESH,
        )

    places = []
    for i in range(blocks):
        source = blocks * row + i
        carries = core == lax.rem(source, 2)
        start = source // 2
        up = carries & (chip >= start) & (chip < last)
        down = carries & (chip <= start) & (chip > 0)
        places.append((source, carries, start, up, down))

    def pass_on(i, m):
        _, _, _, up, down = places[i]

        @pl.when(up)
        def _():
            hand(i, m, 0, jnp.minimum(col + 2, n_col - 1)).start()

        @pl.when(down)
        def _():
            hand(i, m, 1, jnp.maximum(col - 2, 0)).start()

        hand(i, m, 2, partner).start()

    def begin(m):
        for i in range(blocks):

            @pl.when(col == places[i][0])
            def _(i=i):
                wide_ref[:, pl.ds(i * width + place(m), piece)] = total_ref[:, pl.ds(place(m), piece)]
                pass_on(i, m)

    if streamed:
        begin(0)
        begin(1)
    for k in range(1, n_row):
        source = lax.rem(row + n_row - k, n_row)
        pltpu.make_async_remote_copy(
            src_ref=mine,
            dst_ref=chunk(total_ref, source),
            send_sem=ag_send.at[k - 1],
            recv_sem=ag_recv.at[k - 1],
            device_id={"row": source},
            device_id_type=MESH,
        ).wait_recv()
        if streamed:
            begin(2 * k)
            begin(2 * k + 1)
    if not streamed:
        for m in range(pieces):
            begin(m)

    def follow(i, m, chosen):
        @pl.when(chosen)
        def _():
            hand(i, m, 2, partner).wait_recv()
            pass_on(i, m)

    nearest = []
    for i in range(blocks):
        _, carries, start, _, _ = places[i]
        nearest.append(carries & ((chip == start + 1) | (chip == start - 1)))
        follow(i, 0, nearest[i])

    total = total_ref[...]
    gram = dot(total, total if own else other_ref[...], ((1,), (1,)), highest)
    top = jnp.where(col == 0, total[:, B : 2 * B], 0.0)
    smalls[0] = jnp.concatenate([gram, top], axis=1)
    sends = []
    for k in range(1, n_col):
        copy = pltpu.make_async_remote_copy(
            src_ref=smalls.at[0],
            dst_ref=smalls.at[k],
            send_sem=sm_send.at[k - 1],
            recv_sem=sm_recv.at[k - 1],
            device_id={"col": lax.rem(col + k, n_col)},
            device_id_type=MESH,
        )
        copy.start()
        sends.append(copy)

    for m in range(pieces):
        for i in range(blocks):
            rest = places[i][1] & (col != places[i][0])
            follow(i, m, rest & jnp.logical_not(nearest[i]) if m == 0 else rest)

    for copy in sends:
        copy.wait_recv()
    small_ref[...] = jnp.zeros_like(small_ref)

    def add_small(j, carry):
        slot = lax.rem(col + n_col - j, n_col)
        small_ref[...] += smalls[slot]
        return carry

    lax.fori_loop(0, n_col, add_small, 0)
    for i in range(blocks):
        _, carries, _, up, down = places[i]
        for m in range(pieces):

            @pl.when(jnp.logical_not(carries))
            def _(i=i, m=m):
                hand(i, m, 2, partner).wait_recv()

            @pl.when(up)
            def _(i=i, m=m):
                hand(i, m, 0, partner).wait_send()

            @pl.when(down)
            def _(i=i, m=m):
                hand(i, m, 1, partner).wait_send()

            @pl.when(carries)
            def _(i=i, m=m):
                hand(i, m, 2, partner).wait_send()

    for copy in scatters + gathers + sends:
        copy.wait_send()


def exchange(n_row, n_col, identifier, part, other=None):
    width = part.shape[1]
    blocks = n_col // n_row
    pieces = min(2 * n_row, 8, width // 128)
    lane_parts = math.gcd(n_row, width // 128)
    chunk = (B * lane_parts // n_row, width // lane_parts)
    dma = pltpu.SemaphoreType.DMA
    args = (part,) if other is None else (part, other)
    whole = pl.BlockSpec(memory_space=pltpu.VMEM)
    return pl.pallas_call(
        functools.partial(exchange_kernel, n_row, n_col, blocks, pieces, other is None),
        out_shape=(
            jax.ShapeDtypeStruct((B, width), jnp.float32),
            jax.ShapeDtypeStruct((B, blocks * width), jnp.float32),
            jax.ShapeDtypeStruct((B, 2 * B), jnp.float32),
        ),
        in_specs=[whole] * len(args),
        out_specs=(whole,) * 3,
        scratch_shapes=[
            pltpu.VMEM((n_row - 1,) + chunk, jnp.float32),
            pltpu.VMEM((n_col, B, 2 * B), jnp.float32),
            dma((n_row - 1,)),
            dma((n_row - 1,)),
            dma((n_row - 1,)),
            dma((n_row - 1,)),
            dma((n_col - 1,)),
            dma((n_col - 1,)),
            dma((3, blocks, pieces)),
            dma((blocks, pieces)),
        ],
        compiler_params=pltpu.CompilerParams(
            collective_id=identifier, has_side_effects=True, vmem_limit_bytes=24 << 20
        ),
    )(*args)


def on_device(n_row, n_col, matrix):
    rows_dev, cols_dev = matrix.shape
    first_row = lax.axis_index("row") == 0
    first_col = lax.axis_index("col") == 0
    after = first_row & (
        lax.axis_index("col") * cols_dev + jnp.arange(cols_dev, dtype=jnp.int32) >= B
    )
    share = functools.partial(exchange, n_row, n_col)
    panel_cols, panel_rows, small = share(0, jnp.where(after[None, :], matrix[:B, :], 0.0))
    small = jnp.concatenate([small[:, :B], small[:, B:].T], axis=1)
    upper, inner = factor(small)
    lower = upper.T
    basis_rows = panel_rows.at[:, B : 2 * B].add(jnp.where(first_row, lower, 0.0))
    basis_cols = panel_cols.at[:, B : 2 * B].add(jnp.where(first_col, lower, 0.0))
    image_part = dot(basis_rows, matrix, ((1,), (0,)))
    image_cols, image_rows, small = share(1, image_part, basis_cols)
    core = small[:, :B]
    middle = 0.5 * dot(inner, dot(core, inner, ((1,), (0,)), highest), ((0,), (0,)), highest)

    def updates(image, basis):
        return dot(inner, image, ((0,), (0,))) - dot(middle, basis, ((0,), (0,)))

    lefts = jnp.concatenate([basis_rows, updates(image_rows, basis_rows)], axis=0)
    rights = jnp.concatenate([updates(image_cols, basis_cols), basis_cols], axis=0)
    return matrix - dot(lefts, rights, ((0,), (0,)))


def solution(mesh):
    placed = (P("row", "col"),)
    return jax.shard_map(
        functools.partial(on_device, mesh.shape["row"], mesh.shape["col"]),
        mesh=mesh,
        in_specs=placed,
        out_specs=P("row", "col"),
        check_vma=False,
    )
```
